512 devices in a mesh: los: 16 (over z_hi, y), sky: 32 (over x, z_lo, core).
Axes of the slice: x: 4, y: 8, z: 8 (z_hi: 2, z_lo: 4; z = z_hi * 4 + z_lo), core: 2. Of those that a mesh axis runs over, the one named last changes fastest.
Arguments:
- state: float32 [12, 524288], P(None, ('los', 'sky')), may hold values from -6 to 6
- deflection: bfloat16 [16, 2, 64, 8192], P('los', None, None, 'sky'), may hold values from -6 to 6
- shear: bfloat16 [16, 2, 96, 8192], P('los', None, None, 'sky'), may hold values from -3 to 3
- routes: int32 [4, 2, 524288, 1], P(None, None, ('los', 'sky')), may hold values from 0 to 31; in each aligned block of 1024 rows (0 to 1023, 1024 to 2047, ..., all dimensions but the last counted through in order) at most 64 rows name the same one
- patches: int32 [4, 2, 524288], P(None, None, ('los', 'sky')), may hold values from 0 to 255
Outputs:
- traced: float32 [12, 524288], P(None, ('los', 'sky'))
The draws below stay inside these ranges and needn't reach their ends.
Inputs may be any that keep to these rules, and one draw needn't show every extreme that they name: `routes`: in each hop and plane, one device's 1024 slots name one tile at most 64 times, and exactly 64 times in some.
All inputs are finite; a program needn't handle non-finite values.
Results may differ from the reference program's by a relative error of at most 0.0003.
Values sent between devices are 32-bit elements; how exact they have to be, the bound alone decides.
No kernel may reach another device: no remote copies, remote signals or barrier semaphores. Data moves between devices by JAX's collectives and lax.ppermute only.
A program may use at most 64 MiB of HBM per device.

```python
import math
import jax
import jax.numpy as jnp
import numpy as np
from jax import lax

RAYS_DEV = 1024
PATCHES = 256
HOPS = 4
CAP = 64
TOTAL_RAYS = 524288
N_LOS = 16
N_SKY = 32


def with_ends(entries, own_key, least, largest):
    place = [jax.random.randint(jax.random.fold_in(own_key, axis), (), 0, length) for axis, length in enumerate(entries.shape)]
    main_axis = entries.shape.index(max(entries.shape))
    beside = place[:main_axis] + [(place[main_axis] + 1) % entries.shape[main_axis]] + place[main_axis + 1:]
    return entries.at[tuple(place)].set(least).at[tuple(beside)].set(largest)


def steps_of(own_key, shape, cuts, least, largest):
    def one(position, shards_of):
        steps = jax.random.uniform(jax.random.fold_in(jax.random.fold_in(own_key, 6), position), (shards_of,), jnp.float32, least / len(cuts), largest / len(cuts))
        return jnp.repeat(jnp.exp(steps), shape[position] // shards_of).reshape((-1,) + (1,) * (len(shape) - position - 1))

    level = one(*cuts[0])
    for cut in cuts[1:]:
        level = level * one(*cut)
    return level


def shared_out(rng, own, number, rows, amount, top, bound, slope):
    order = jax.random.permutation(rng, amount)
    heavy_load, ordinary = portions_of(amount, rows * top, bound, slope, True), portions_of(amount, rows * top, bound, slope, False)
    places = jnp.arange(amount)

    def named(tallies, turn):
        used = int((tallies > 0).sum())
        fixed = max(1, used // 4)
        passed = fixed + (places - fixed + turn * (used - fixed)) % max(1, amount - fixed)
        return jnp.zeros((amount,), jnp.int32).at[order[jnp.where(places < fixed, places, passed)]].set(jnp.asarray(tallies, jnp.int32))

    tallies = jnp.where(number % 4 == 0, named(heavy_load, number // 4), named(ordinary, number - number // 4 - 1))
    mixed = jax.random.permutation(jax.random.fold_in(own, 3), amount)
    source_of, receiver = mixed[0:amount // 2 * 2:2], mixed[1:amount // 2 * 2:2]
    room = jnp.minimum(tallies[source_of] - 1, bound - tallies[receiver]) // 2
    room = jnp.where((source_of == order[0]) | (receiver == order[0]) | (tallies[receiver] == 0), 0, jnp.maximum(room, 0))
    passed = jax.random.randint(jax.random.fold_in(own, 4), (amount // 2,), 0, 1 << 20) % (room + 1)
    tallies = tallies.at[source_of].add(-passed).at[receiver].add(passed)
    items = jnp.searchsorted(jnp.cumsum(tallies), jnp.arange(rows * top), side="right").astype(jnp.int32)
    listing = items.reshape(top, rows).T
    listing = listing[jax.random.permutation(jax.random.fold_in(own, 1), rows)]
    turn = jax.random.randint(jax.random.fold_in(own, 2), (rows, 1), 0, top)
    return jnp.take_along_axis(listing, (jnp.arange(top)[None, :] + turn) % top, axis=1)


def portions_of(amount, total, most, lean, full):
    weights = [(1 << 20) // math.isqrt(rank ** lean) + 1 for rank in range(1, amount + 1)]
    largest = most if full else min(most, max(-(-total // amount), total * weights[0] // sum(weights)))
    least = 1 if total - largest >= amount - 1 else 0
    counts, rest = [largest] + [least] * (amount - 1), total - largest - least * (amount - 1)
    while rest > 0:
        movable = [i for i in range(1, amount) if counts[i] < largest] or [i for i in range(1, amount) if counts[i] < most]
        pool, remaining = sum([weights[i] for i in movable]), rest
        for i in movable:
            extra = min(most - counts[i], max(1, remaining * weights[i] // pool), rest)
            counts[i] = counts[i] + extra
            rest = rest - extra
    return np.array(counts)


def noise(rng, dims, width, most, cuts=(), kind=jnp.bfloat16):
    factor_of = steps_of(rng, dims, cuts, -0.22, 0.18) if cuts else 1.0
    values = jax.random.normal(rng, dims, jnp.float32) * width * factor_of
    return jnp.minimum(jnp.maximum(values, -most), most).astype(kind)


def setup_inputs(seed: int = 0) -> dict:
    splits = jax.random.split(jax.random.key(seed), 6)
    state = noise(splits[0], (12, TOTAL_RAYS), 1.0, 6.0, ((1, 512),), jnp.float32)
    deflection = noise(splits[1], (N_LOS, 2, 64, N_SKY * PATCHES), 1.0, 6.0, ((0, 16), (3, 32)))
    shear = noise(splits[2], (N_LOS, 2, 96, N_SKY * PATCHES), 0.5, 3.0, ((0, 16), (3, 32)))
    routes_keys = jax.random.split(jax.random.fold_in(splits[3], 1), HOPS * 2 * TOTAL_RAYS // RAYS_DEV)
    routes_turns = jax.random.permutation(jax.random.fold_in(splits[3], 3), HOPS * 2 * TOTAL_RAYS // RAYS_DEV)
    routes = jax.vmap(lambda own, number: shared_out(jax.random.fold_in(splits[3], 2), own, number, RAYS_DEV, N_SKY, 1, CAP, 2))(routes_keys, routes_turns).reshape((HOPS, 2, TOTAL_RAYS, 1))
    patches = with_ends(jax.random.randint(splits[4], (HOPS, 2, TOTAL_RAYS), 0, PATCHES), jax.random.fold_in(splits[4], 1), 0, PATCHES - 1).astype(jnp.int32)
    return dict(state=state, deflection=deflection, shear=shear, routes=routes, patches=patches)


def weights(pos_x, pos_y):
    across = jnp.arange(4).astype(pos_x.dtype)
    along = jnp.arange(8).astype(pos_x.dtype)
    kern_x = (1.0 + jnp.cos(2.0 * math.pi * (pos_x[None, :] - across[:, None]) / 4.0)) / 4.0
    kern_y = (1.0 + jnp.cos(2.0 * math.pi * (pos_y[None, :] - along[:, None]) / 8.0)) / 8.0
    return (kern_x[:, None, :] * kern_y[None, :, :]).reshape(32, -1)


def interpolate(raw, pos_x, pos_y):
    table = weights(pos_x, pos_y)
    return jnp.sum(raw.reshape(5, 32, -1) * table[None], axis=1)


def advance(current, values):
    pos_x, pos_y, ang_x, ang_y, a11, a12, a21, a22, b11, b12, b21, b22 = [current[k] for k in range(12)]
    alpha_x, alpha_y, psi11, psi12, psi22 = [values[k] for k in range(5)]
    ang_x = ang_x - alpha_x
    ang_y = ang_y - alpha_y
    b11 = b11 - (psi11 * a11 + psi12 * a21)
    b12 = b12 - (psi11 * a12 + psi12 * a22)
    b21 = b21 - (psi12 * a11 + psi22 * a21)
    b22 = b22 - (psi12 * a12 + psi22 * a22)
    pos_x = pos_x + 0.5 * ang_x
    pos_y = pos_y + 0.5 * ang_y
    a11 = a11 + 0.5 * b11
    a12 = a12 + 0.5 * b12
    a21 = a21 + 0.5 * b21
    a22 = a22 + 0.5 * b22
    return jnp.stack([pos_x, pos_y, ang_x, ang_y, a11, a12, a21, a22, b11, b12, b21, b22])


def reference(state, deflection, shear, routes, patches):
    slab_rays = N_SKY * RAYS_DEV
    current = state.reshape(12, N_LOS, slab_rays).transpose(1, 0, 2)
    for hop in range(HOPS):
        for plane in range(2):
            dest = routes[hop, plane, :, 0].reshape(N_LOS, slab_rays)
            which = patches[hop, plane].reshape(N_LOS, slab_rays)

            def one_slab(items, plane=plane):
                rays, defl, shr, tile, patch = items
                fields = jnp.concatenate([defl[plane], shr[plane]], axis=0).astype(jnp.float32)
                column = (tile * PATCHES + patch).astype(jnp.int32)
                raw = jnp.take(fields, column, axis=1)
                return advance(rays, interpolate(raw, rays[0], rays[1]))

            current = lax.map(one_slab, (current, deflection, shear, dest, which))
        current = jnp.roll(current, 1, axis=0)
    return current.transpose(1, 0, 2).reshape(12, -1)
```

```python
import functools
import math

import jax
import jax.numpy as jnp
from jax import lax
from jax.experimental import pallas as pl
from jax.experimental.pallas import tpu as pltpu
from jax.sharding import PartitionSpec as P

RAYS = 1024
PATCHES = 256
HOPS = 4
TILES = 32
ROWS = 48
CHUNK = 256
GROUPS = RAYS // 128
VMEM = pl.BlockSpec(memory_space=pltpu.VMEM)
SMEM = pl.BlockSpec(memory_space=pltpu.SMEM)
PARAMS = pltpu.CompilerParams(vmem_limit_bytes=48 * 1024 * 1024)


def partner(axis, mask):
    shift = {"x": 3, "z": 1, "core": 0}[axis]
    return [(s, s ^ (mask << shift)) for s in range(TILES)]


def coefficients_kernel(defl_ref, shear_ref, out_ref):
    angle = lax.broadcasted_iota(jnp.int32, (8, PATCHES), 0)
    root = math.sqrt(0.5)
    cos_y, sin_y = jnp.zeros((8, PATCHES), jnp.float32), jnp.zeros((8, PATCHES), jnp.float32)
    for j, (c, s) in enumerate(
        [(1, 0), (root, root), (0, 1), (-root, root), (-1, 0), (-root, -root), (0, -1), (root, -root)]
    ):
        cos_y = jnp.where(angle == j, c, cos_y)
        sin_y = jnp.where(angle == j, s, sin_y)
    for plane in range(2):
        for k in range(5):
            source, first = (defl_ref, k * 32) if k < 2 else (shear_ref, (k - 2) * 32)
            cells = source[0, plane, first : first + 32, :].astype(jnp.float32) * (1.0 / 32.0)
            r0, r1, r2, r3 = [cells[i * 8 : i * 8 + 8] for i in range(4)]
            for a, part in enumerate((r0 + r1 + r2 + r3, r0 - r2, r1 - r3)):
                row = plane * ROWS + k * 9 + a * 3
                out_ref[row : row + 1, :] = jnp.sum(part, axis=0, keepdims=True)
                out_ref[row + 1 : row + 2, :] = jnp.sum(part * cos_y, axis=0, keepdims=True)
                out_ref[row + 2 : row + 3, :] = jnp.sum(part * sin_y, axis=0, keepdims=True)
        out_ref[plane * ROWS + 45 : plane * ROWS + 48, :] = jnp.zeros((3, PATCHES), jnp.float32)


def coefficients(deflection, shear):
    return pl.pallas_call(
        coefficients_kernel,
        out_shape=jax.ShapeDtypeStruct((2 * ROWS, PATCHES), jnp.float32),
        in_specs=[VMEM] * 2,
        out_specs=VMEM,
        name="coefficients",
    )(deflection, shear)


def find_rows(hop, table_ref, rel_ref, patch_ref, out_ref):
    for plane in range(2):
        for chunk in range(RAYS // CHUNK):
            lanes = slice(chunk * CHUNK, (chunk + 1) * CHUNK)
            row = hop * 2 + plane
            patch = patch_ref[row : row + 1, lanes]
            rel = rel_ref[row : row + 1, lanes]
            onehot = lax.broadcasted_iota(jnp.int32, (PATCHES, CHUNK), 0) == patch
            onehot = jnp.where(onehot, 1.0, 0.0).astype(jnp.bfloat16)
            onehot = jnp.concatenate([onehot, onehot], axis=0)
            found = jnp.dot(table_ref[plane], onehot, preferred_element_type=jnp.float32)
            total = [jnp.zeros((8, CHUNK), jnp.float32) for _ in range(ROWS // 8)]
            wide = jnp.broadcast_to(rel, (8, CHUNK))
            for tile in range(TILES):
                here = wide == tile
                for part in range(ROWS // 8):
                    first = tile * ROWS + part * 8
                    total[part] = total[part] + jnp.where(here, found[first : first + 8], 0.0)
            for part in range(ROWS // 8):
                for half in range(CHUNK // 128):
                    group = chunk * (CHUNK // 128) + half
                    first = (plane * ROWS + part * 8) * GROUPS + group
                    out_ref[pl.ds(first, 8, stride=GROUPS), :] = total[part][:, half * 128 : half * 128 + 128]


def first_lookup_kernel(own_ref, other_ref, rel_ref, patch_ref, out_ref, table_ref):
    for core, ref in enumerate((own_ref, other_ref)):
        for block in range(TILES // 2):
            tile = block * 2 + core
            for plane in range(2):
                values = ref[block, plane * ROWS : (plane + 1) * ROWS, :]
                high = values.astype(jnp.bfloat16)
                low = (values - high.astype(jnp.float32)).astype(jnp.bfloat16)
                table_ref[plane, tile * ROWS : (tile + 1) * ROWS, :PATCHES] = high
                table_ref[plane, tile * ROWS : (tile + 1) * ROWS, PATCHES:] = low
    find_rows(0, table_ref, rel_ref, patch_ref, out_ref)


COST = pl.CostEstimate(flops=2 * 2 * TILES * ROWS * 512 * RAYS, bytes_accessed=4 * 1024 * 1024, transcendentals=0)
FOUND = jax.ShapeDtypeStruct((2 * ROWS * GROUPS, 128), jnp.float32)


def first_lookup(own, other, rel, patch):
    return pl.pallas_call(
        first_lookup_kernel,
        out_shape=(FOUND, jax.ShapeDtypeStruct((2, TILES * ROWS, 2 * PATCHES), jnp.bfloat16)),
        in_specs=[VMEM] * 4,
        out_specs=(VMEM, VMEM),
        compiler_params=PARAMS,
        cost_estimate=COST,
        name="first_lookup",
    )(own, other, rel, patch)


def lookup(hop, table, rel, patch):
    return pl.pallas_call(
        functools.partial(find_rows, hop),
        out_shape=FOUND,
        in_specs=[VMEM] * 3,
        out_specs=VMEM,
        compiler_params=PARAMS,
        cost_estimate=COST,
        name="lookup",
    )(table, rel, patch)


def sine(turn):
    v = turn * (2.0 * math.pi)
    v2 = v * v
    poly = 1.0 / 6227020800.0
    for c in (-1.0 / 39916800.0, 1.0 / 362880.0, -1.0 / 5040.0, 1.0 / 120.0, -1.0 / 6.0):
        poly = poly * v2 + c
    return v + v * v2 * poly


def wave(turns):
    t = turns - jnp.floor(turns + 0.5)
    size = jnp.abs(t)
    fold = jnp.where(t >= 0, 0.5 - t, -0.5 - t)
    return sine(0.25 - size), sine(jnp.where(size > 0.25, fold, t))


def advance(state, read):
    pos_x, pos_y, ang_x, ang_y, a11, a12, a21, a22, b11, b12, b21, b22 = state
    cos_x, sin_x = wave(pos_x * 0.25)
    cos_y, sin_y = wave(pos_y * 0.125)
    values = []
    for k in range(5):
        parts = []
        for a in range(3):
            m = [read(k * 9 + a * 3 + b) for b in range(3)]
            parts.append(m[0] + m[1] * cos_y + m[2] * sin_y)
        values.append(parts[0] + parts[1] * cos_x + parts[2] * sin_x)
    alpha_x, alpha_y, psi11, psi12, psi22 = values
    ang_x = ang_x - alpha_x
    ang_y = ang_y - alpha_y
    b11 = b11 - (psi11 * a11 + psi12 * a21)
    b12 = b12 - (psi11 * a12 + psi12 * a22)
    b21 = b21 - (psi12 * a11 + psi22 * a21)
    b22 = b22 - (psi12 * a12 + psi22 * a22)
    pos_x = pos_x + 0.5 * ang_x
    pos_y = pos_y + 0.5 * ang_y
    a11 = a11 + 0.5 * b11
    a12 = a12 + 0.5 * b12
    a21 = a21 + 0.5 * b21
    a22 = a22 + 0.5 * b22
    return [pos_x, pos_y, ang_x, ang_y, a11, a12, a21, a22, b11, b12, b21, b22]


def step_kernel(step, q_ref, *refs):
    *refs, out_ref = refs
    q = q_ref[0]
    refs = list(refs)
    main_ref = refs.pop(0)
    wrap_ref = refs.pop(0) if step >= 2 else None
    early_ref = refs.pop(0) if step < HOPS else None
    late_ref = refs.pop(0) if step >= 2 else None
    shape = (GROUPS, 128)
    late = jnp.full(shape, q, jnp.int32) < step
    crossed = jnp.full(shape, q, jnp.int32) == 0

    def rows(ref, k):
        return ref[k * GROUPS : (k + 1) * GROUPS, :]

    state = [rows(main_ref, k) for k in range(12)]
    if wrap_ref is not None:
        state = [jnp.where(crossed, rows(wrap_ref, k), state[k]) for k in range(12)]
    for plane in range(2):

        def read(k, plane=plane):
            k = plane * ROWS + k
            if early_ref is None:
                return rows(late_ref, k)
            if late_ref is None:
                return rows(early_ref, k)
            return jnp.where(late, rows(late_ref, k), rows(early_ref, k))

        state = advance(state, read)
    for k in range(12):
        out_ref[k * GROUPS : (k + 1) * GROUPS, :] = state[k]


def run_step(step, q, main, wrap, found):
    args = [main]
    if step >= 2:
        args.append(wrap)
    if step < HOPS:
        args.append(found[step])
    if step >= 2:
        args.append(found[step - 1])
    return pl.pallas_call(
        functools.partial(step_kernel, step),
        out_shape=jax.ShapeDtypeStruct((12 * GROUPS, 128), jnp.float32),
        in_specs=[SMEM] + [VMEM] * len(args),
        out_specs=VMEM,
        cost_estimate=pl.CostEstimate(flops=400 * RAYS, bytes_accessed=500 * 1024, transcendentals=0),
        name="step",
    )(q, *args)


def gather_tables(own):
    column = jnp.stack([own] + [lax.ppermute(own, "sky", partner("z", m)) for m in (1, 2, 3)])
    whole = jnp.concatenate([column] + [lax.ppermute(column, "sky", partner("x", m)) for m in (1, 2, 3)])
    return whole, lax.ppermute(whole, "sky", partner("core", 1))


def body(state, deflection, shear, routes, patches):
    slabs = lax.axis_size("los")
    run = slabs // 2
    slab = lax.axis_index("los")
    q = (slab % run).astype(jnp.int32).reshape(1)
    onward = [(i, i + 1) for i in range(slabs - 1) if i % run != run - 1]
    across = [(i, (i + 1) % slabs) for i in range(slabs) if i % run == run - 1]

    own = coefficients(deflection, shear)
    whole, other = gather_tables(own)
    rel = jnp.bitwise_xor(routes.reshape(2 * HOPS, RAYS), lax.axis_index("sky").astype(jnp.int32))
    patch = patches.reshape(2 * HOPS, RAYS)
    found = [None] * HOPS
    found[0], table = first_lookup(whole, other, rel, patch)
    main, wraps = state.reshape(12 * GROUPS, 128), []
    for step in range(HOPS + 1):
        if 0 < step < HOPS:
            found[step] = lookup(step, table, rel, patch)
        moved = run_step(step, q, main, wraps[step - 2] if step >= 2 else None, found)
        arrived = lax.ppermute(moved, "los", onward)
        if step < HOPS:
            wraps.append(lax.ppermute(moved, "los", across))
        before, main = main, arrived
    out = jnp.where(q[0] == 0, wraps[HOPS - 1], jnp.where(q[0] < HOPS, main, before))
    return out.reshape(12, RAYS)


def solution(mesh):
    placed = (
        P(None, ("los", "sky")),
        P("los", None, None, "sky"),
        P("los", None, None, "sky"),
        P(None, None, ("los", "sky"), None),
        P(None, None, ("los", "sky")),
    )
    return jax.shard_map(
        body, mesh=mesh, in_specs=placed, out_specs=P(None, ("los", "sky")), check_vma=False
    )
```

```python
import functools
import math

import jax
import jax.numpy as jnp
from jax import lax
from jax.experimental import pallas as pl
from jax.experimental.pallas import tpu as pltpu
from jax.sharding import PartitionSpec as P

RAYS = 1024
PATCHES = 256
HOPS = 4
TILES = 32
ROWS = 48
CHUNK = 256
GROUPS = RAYS // 128
VMEM = pl.BlockSpec(memory_space=pltpu.VMEM)
SMEM = pl.BlockSpec(memory_space=pltpu.SMEM)
SMALL = pltpu.CompilerParams(vmem_limit_bytes=4 * 1024 * 1024)
LARGE = pltpu.CompilerParams(vmem_limit_bytes=12 * 1024 * 1024)


def partner(axis, mask):
    shift = {"x": 3, "z": 1, "core": 0}[axis]
    return [(s, s ^ (mask << shift)) for s in range(TILES)]


def coefficients_kernel(defl_hbm, shear_hbm, out_ref, defl_ref, shear_ref, defl_sem, shear_sem):
    copies = (
        pltpu.make_async_copy(defl_hbm, defl_ref, defl_sem),
        pltpu.make_async_copy(shear_hbm, shear_ref, shear_sem),
    )
    for copy in copies:
        copy.start()
    for copy in copies:
        copy.wait()
    angle = lax.broadcasted_iota(jnp.int32, (8, PATCHES), 0)
    root = math.sqrt(0.5)
    cos_y, sin_y = jnp.zeros((8, PATCHES), jnp.float32), jnp.zeros((8, PATCHES), jnp.float32)
    for j, (c, s) in enumerate(
        [(1, 0), (root, root), (0, 1), (-root, root), (-1, 0), (-root, -root), (0, -1), (root, -root)]
    ):
        cos_y = jnp.where(angle == j, c, cos_y)
        sin_y = jnp.where(angle == j, s, sin_y)
    for plane in range(2):
        for k in range(5):
            source, first = (defl_ref, k * 32) if k < 2 else (shear_ref, (k - 2) * 32)
            cells = source[0, plane, first : first + 32, :].astype(jnp.float32) * (1.0 / 32.0)
            r0, r1, r2, r3 = [cells[i * 8 : i * 8 + 8] for i in range(4)]
            for a, part in enumerate((r0 + r1 + r2 + r3, r0 - r2, r1 - r3)):
                row = plane * ROWS + k * 9 + a * 3
                out_ref[row : row + 1, :] = jnp.sum(part, axis=0, keepdims=True)
                out_ref[row + 1 : row + 2, :] = jnp.sum(part * cos_y, axis=0, keepdims=True)
                out_ref[row + 2 : row + 3, :] = jnp.sum(part * sin_y, axis=0, keepdims=True)
        out_ref[plane * ROWS + 45 : plane * ROWS + 48, :] = jnp.zeros((3, PATCHES), jnp.float32)


def coefficients(deflection, shear):
    return pl.pallas_call(
        coefficients_kernel,
        out_shape=jax.ShapeDtypeStruct((2 * ROWS, PATCHES), jnp.float32),
        in_specs=[pl.BlockSpec(memory_space=pltpu.HBM)] * 2,
        out_specs=VMEM,
        scratch_shapes=[
            pltpu.VMEM(deflection.shape, deflection.dtype),
            pltpu.VMEM(shear.shape, shear.dtype),
            pltpu.SemaphoreType.DMA,
            pltpu.SemaphoreType.DMA,
        ],
        compiler_params=SMALL,
        name="coefficients",
    )(*[pltpu.with_memory_space_constraint(a, pltpu.HBM) for a in (deflection, shear)])


def join_kernel(count, *refs):
    out_ref, place = refs[-1], 0
    for ref in refs[:count]:
        out_ref[place : place + ref.shape[0]] = ref[...]
        place += ref.shape[0]


def join(blocks, after=()):
    shape = (sum(b.shape[0] for b in blocks), *blocks[0].shape[1:])
    return pl.pallas_call(
        functools.partial(join_kernel, len(blocks)),
        out_shape=jax.ShapeDtypeStruct(shape, blocks[0].dtype),
        in_specs=[VMEM] * (len(blocks) + len(after)),
        out_specs=VMEM,
        compiler_params=SMALL,
        name="join",
    )(*blocks, *after)


def fill_table(sources, table_ref, count):
    place = 0
    for ref in sources:
        for block in range(max(0, ref.shape[0] - count), ref.shape[0]):
            for plane in range(2):
                values = ref[block, plane * ROWS : (plane + 1) * ROWS, :]
                high = values.astype(jnp.bfloat16)
                low = (values - high.astype(jnp.float32)).astype(jnp.bfloat16)
                table_ref[plane, place * ROWS : (place + 1) * ROWS, :PATCHES] = high
                table_ref[plane, place * ROWS : (place + 1) * ROWS, PATCHES:] = low
            place += 1


def find_rows(hop, tiles, table_ref, rel_ref, patch_ref, out_ref, before_ref=None):
    for plane in range(2):
        for chunk in range(RAYS // CHUNK):
            lanes = slice(chunk * CHUNK, (chunk + 1) * CHUNK)
            row = hop * 2 + plane
            patch = patch_ref[row : row + 1, lanes]
            rel = rel_ref[row : row + 1, lanes]
            onehot = lax.broadcasted_iota(jnp.int32, (PATCHES, CHUNK), 0) == patch
            onehot = jnp.where(onehot, 1.0, 0.0).astype(jnp.bfloat16)
            onehot = jnp.concatenate([onehot, onehot], axis=0)
            found = jnp.dot(table_ref[plane, : len(tiles) * ROWS], onehot, preferred_element_type=jnp.float32)
            total = [jnp.zeros((8, CHUNK), jnp.float32) for _ in range(ROWS // 8)]
            wide = jnp.broadcast_to(rel, (8, CHUNK))
            for place, tile in enumerate(tiles):
                here = wide == tile
                for part in range(ROWS // 8):
                    first = place * ROWS + part * 8
                    total[part] = total[part] + jnp.where(here, found[first : first + 8], 0.0)
            for part in range(ROWS // 8):
                for half in range(CHUNK // 128):
                    group = chunk * (CHUNK // 128) + half
                    first = (plane * ROWS + part * 8) * GROUPS + group
                    place = pl.ds(first, 8, stride=GROUPS)
                    sums = total[part][:, half * 128 : half * 128 + 128]
                    out_ref[place, :] = sums if before_ref is None else sums + before_ref[place, :]


def table_kernel(*refs):
    fill_table(refs[:-1], refs[-1], TILES)


def table_of(sources):
    count = sum(source.shape[0] for source in sources)
    return pl.pallas_call(
        table_kernel,
        out_shape=jax.ShapeDtypeStruct((2, count * ROWS, 2 * PATCHES), jnp.bfloat16),
        in_specs=[VMEM] * len(sources),
        out_specs=VMEM,
        compiler_params=LARGE,
        name="table",
    )(*sources)


def lookup_kernel(hops, tiles, count, blocks, added, *refs):
    sources, (rel_ref, patch_ref), refs = refs[:count], refs[count : count + 2], refs[count + 2 :]
    before = refs[: len(hops)] if added else [None] * len(hops)
    outs = refs[-len(hops) :]
    if blocks:
        *outs, table_ref = refs[-1 - len(hops) :]
        fill_table(sources, table_ref, blocks)
    else:
        (table_ref,) = sources
    for hop, before_ref, out_ref in zip(hops, before, outs, strict=True):
        find_rows(hop, tiles, table_ref, rel_ref, patch_ref, out_ref, before_ref)


FOUND = jax.ShapeDtypeStruct((2 * ROWS * GROUPS, 128), jnp.float32)


COSTLY = pl.CostEstimate(flops=4000000000, bytes_accessed=100000, transcendentals=0)
COSTLIER = pl.CostEstimate(flops=16000000000, bytes_accessed=100000, transcendentals=0)
COST = pl.CostEstimate(flops=100000, bytes_accessed=100000, transcendentals=0)


def scratch_table(tiles):
    return pltpu.VMEM((2, len(tiles) * ROWS, 2 * PATCHES), jnp.bfloat16)


def lookup(hops, tiles, sources, rel, patch, before=(), blocks=TILES):
    first = len(sources) + 2
    return pl.pallas_call(
        functools.partial(lookup_kernel, hops, tiles, len(sources), blocks, bool(before)),
        out_shape=[FOUND] * len(hops),
        in_specs=[VMEM] * (first + len(before)),
        out_specs=[VMEM] * len(hops),
        input_output_aliases={first + i: i for i in range(len(before))},
        scratch_shapes=[scratch_table(tiles)] if blocks else [],
        compiler_params=LARGE,
        cost_estimate=COSTLIER if blocks else COST if hops[0] == 1 else COST,
        name="lookup",
    )(*sources, rel, patch, *before)


def sine(turn):
    v = turn * (2.0 * math.pi)
    v2 = v * v
    poly = 1.0 / 6227020800.0
    for c in (-1.0 / 39916800.0, 1.0 / 362880.0, -1.0 / 5040.0, 1.0 / 120.0, -1.0 / 6.0):
        poly = poly * v2 + c
    return v + v * v2 * poly


def wave(turns):
    t = turns - jnp.floor(turns + 0.5)
    size = jnp.abs(t)
    fold = jnp.where(t >= 0, 0.5 - t, -0.5 - t)
    return sine(0.25 - size), sine(jnp.where(size > 0.25, fold, t))


def advance(state, read):
    pos_x, pos_y, ang_x, ang_y, a11, a12, a21, a22, b11, b12, b21, b22 = state
    cos_x, sin_x = wave(pos_x * 0.25)
    cos_y, sin_y = wave(pos_y * 0.125)
    values = []
    for k in range(5):
        parts = []
        for a in range(3):
            m = [read(k * 9 + a * 3 + b) for b in range(3)]
            parts.append(m[0] + m[1] * cos_y + m[2] * sin_y)
        values.append(parts[0] + parts[1] * cos_x + parts[2] * sin_x)
    alpha_x, alpha_y, psi11, psi12, psi22 = values
    ang_x = ang_x - alpha_x
    ang_y = ang_y - alpha_y
    b11 = b11 - (psi11 * a11 + psi12 * a21)
    b12 = b12 - (psi11 * a12 + psi12 * a22)
    b21 = b21 - (psi12 * a11 + psi22 * a21)
    b22 = b22 - (psi12 * a12 + psi22 * a22)
    pos_x = pos_x + 0.5 * ang_x
    pos_y = pos_y + 0.5 * ang_y
    a11 = a11 + 0.5 * b11
    a12 = a12 + 0.5 * b12
    a21 = a21 + 0.5 * b21
    a22 = a22 + 0.5 * b22
    return [pos_x, pos_y, ang_x, ang_y, a11, a12, a21, a22, b11, b12, b21, b22]


def rows(ref, k):
    return ref[k * GROUPS : (k + 1) * GROUPS, :]


def both_planes(state, read):
    for plane in range(2):
        state = advance(state, lambda k, plane=plane: read(plane * ROWS + k))
    return state


def summed(refs, k):
    return functools.reduce(jnp.add, [rows(ref, k) for ref in refs])


def first_step_kernel(tiles, parts, table_ref, rel_ref, patch_ref, state_ref, *refs):
    part_refs, (out_ref, leaving_ref, found_ref) = refs[:parts], refs[-3:]
    find_rows(0, tiles, table_ref, rel_ref, patch_ref, found_ref)
    found = (*part_refs, found_ref)
    state = both_planes([rows(state_ref, k) for k in range(12)], lambda k: summed(found, k))
    for k in range(12):
        out_ref[k * GROUPS : (k + 1) * GROUPS, :] = state[k]
        leaving_ref[k * GROUPS : (k + 1) * GROUPS, :] = state[k]


MOVED = jax.ShapeDtypeStruct((12 * GROUPS, 128), jnp.float32)
CROSSING = (100,108,108,204)


def moved_out(senders, step):
    return jax.ShapeDtypeStruct((CROSSING[step], 128), jnp.float32) if senders else MOVED


def first_step(tiles, table, rel, patch, state, parts):
    return pl.pallas_call(
        functools.partial(first_step_kernel, tiles, len(parts)),
        out_shape=[MOVED, moved_out(True, 0)],
        in_specs=[VMEM] * (4 + len(parts)),
        out_specs=[VMEM] * 2,
        scratch_shapes=[pltpu.VMEM(FOUND.shape, FOUND.dtype)],
        compiler_params=LARGE,
        cost_estimate=COST,
        name="first_step",
    )(table, rel, patch, state, *parts)


def step_kernel(senders, step, counts, q_ref, *refs):
    out_ref = refs[-1]
    main_ref, *refs = refs[: sum(counts)]
    wrap_ref = refs.pop(0) if counts[1] else None
    early, late = refs[: counts[2]], refs[counts[2] :]
    q = q_ref[0]
    shape = (GROUPS, 128)

    @pl.when((q == RUN - 1) == senders)
    def _():
        behind = jnp.full(shape, q, jnp.int32) < step
        crossed = jnp.full(shape, q, jnp.int32) == 0
        state = [rows(main_ref, k) for k in range(12)]
        if wrap_ref is not None and step > 1:
            state = [jnp.where(crossed, rows(wrap_ref, k), state[k]) for k in range(12)]

        def read(k):
            if not early:
                return summed(late, k)
            if not late:
                return summed(early, k)
            return jnp.where(behind, summed(late, k), summed(early, k))

        state = both_planes(state, read)
        if wrap_ref is not None and step == 1:
            state = [jnp.where(crossed, rows(wrap_ref, k), state[k]) for k in range(12)]
        for k in range(12):
            out_ref[k * GROUPS : (k + 1) * GROUPS, :] = state[k]


def run_step(senders, step, q, main, wrap, found, after=()):
    crossed = [] if senders else [wrap]
    early = found[step : step + 1]
    late = found[step - 1 : step] if step >= 2 and not senders else []
    args = [main, *crossed, *early, *late]
    return pl.pallas_call(
        functools.partial(step_kernel, senders, step, (1, len(crossed), len(early), len(late))),
        out_shape=moved_out(senders, step),
        in_specs=[SMEM] + [VMEM] * (len(args) + len(after)),
        out_specs=VMEM,
        compiler_params=SMALL,
        cost_estimate=COST,
        name="step",
    )(q, *args, *after)


RUN = 8


def tiles_of(masks, core):
    return tuple(m * 8 + j * 2 + core for m in masks for j in range(4))


def mixed(axis_first, axis_second):
    pairs = []
    for s in range(TILES):
        mask = axis_first if s % 2 == 0 else axis_second
        pairs.append((s, s ^ (mask << 3)))
    return pairs


def body(state, deflection, shear, routes, patches):
    slabs = lax.axis_size("los")
    slab = lax.axis_index("los")
    q = (slab % RUN).astype(jnp.int32).reshape(1)
    across = [(i, (i + 1) % slabs) for i in range(slabs) if i % RUN == RUN - 1]

    def onward(step):
        idle = {step} if step < HOPS else set(range(HOPS, RUN))
        return [(i, i + 1) for i in range(slabs) if i % RUN != RUN - 1 and i % RUN not in idle]

    route, patch = routes.reshape(2 * HOPS, RAYS), patches.reshape(2 * HOPS, RAYS)
    rel = jnp.bitwise_xor(route, lax.axis_index("sky").astype(jnp.int32))
    rel = jnp.bitwise_xor(rel, ((rel >> 3) & route & 1) << 4)
    rays = state.reshape(12 * GROUPS, 128)

    own = coefficients(deflection, shear)
    column = [own] + [lax.ppermute(own, "sky", partner("z", m)) for m in (1, 2, 3)]
    column = join([block[None] for block in column], [rel, patch, rays])
    near = [lax.ppermute(column, "sky", mixed(1, 3)), lax.ppermute(column, "sky", mixed(3, 1))]
    far = lax.ppermute(column, "sky", partner("x", 2))

    hops = range(HOPS)
    chip = partner("core", 1)
    found = lookup(hops, tiles_of((0, 1), 0), [column, near[0]], rel, patch)
    found = lookup(hops, tiles_of((3,), 0), [near[1]], rel, patch, found)
    other = [lax.ppermute(join([column, *near], found), "sky", chip), lax.ppermute(far, "sky", chip)]
    found = list(lookup([0], tiles_of((2,), 0), [far], rel, patch, found[:1])) + list(found[1:])
    there = tiles_of((0, 1, 3, 2), 1)
    other = table_of([*other, far])
    moved, leaving = first_step(there, other, rel, patch, rays, found[:1])
    wraps, kept = [lax.ppermute(leaving, "los", across)], moved
    main, before = lax.ppermute(moved, "los", onward(0)), None
    for step in range(1, HOPS + 1):
        if step < HOPS:
            (found[step],) = lookup([step], there + tiles_of((2,), 0), [other], rel, patch, found[step : step + 1], 0)
        after = ()
        if step < HOPS:
            leaving = run_step(True, step, q, main, None, found)
            wraps.append(lax.ppermute(leaving, "los", across))
            after = (leaving,)
        moved = run_step(False, step, q, main, wraps[step - 2] if step >= 2 else kept, found, after)
        main, before = lax.ppermute(moved, "los", onward(step)), main
    out = jnp.where(q[0] == 0, wraps[HOPS - 1][:96], jnp.where(q[0] <= HOPS, main, before))
    return out.reshape(12, RAYS)


def solution(mesh):
    placed = (
        P(None, ("los", "sky")),
        P("los", None, None, "sky"),
        P("los", None, None, "sky"),
        P(None, None, ("los", "sky"), None),
        P(None, None, ("los", "sky")),
    )
    return jax.shard_map(
        body, mesh=mesh, in_specs=placed, out_specs=P(None, ("los", "sky")), check_vma=False
    )
```

```python
import functools
import math

import jax
import jax.numpy as jnp
from jax import lax
from jax.experimental import pallas as pl
from jax.experimental.pallas import tpu as pltpu
from jax.sharding import PartitionSpec as P

RAYS = 1024
PATCHES = 256
HOPS = 4
TILES = 32
ROWS = 48
CHUNK = 256
GROUPS = RAYS // 128
VMEM = pl.BlockSpec(memory_space=pltpu.VMEM)
SMEM = pl.BlockSpec(memory_space=pltpu.SMEM)
SMALL = pltpu.CompilerParams(vmem_limit_bytes=4 * 1024 * 1024)
LARGE = pltpu.CompilerParams(vmem_limit_bytes=12 * 1024 * 1024)


def partner(axis, mask):
    shift = {"x": 3, "z": 1, "core": 0}[axis]
    return [(s, s ^ (mask << shift)) for s in range(TILES)]


def coefficients_kernel(defl_hbm, shear_hbm, out_ref, defl_ref, shear_ref, defl_sem, shear_sem):
    copies = (
        pltpu.make_async_copy(defl_hbm, defl_ref, defl_sem),
        pltpu.make_async_copy(shear_hbm, shear_ref, shear_sem),
    )
    for copy in copies:
        copy.start()
    for copy in copies:
        copy.wait()
    angle = lax.broadcasted_iota(jnp.int32, (8, PATCHES), 0)
    root = math.sqrt(0.5)
    cos_y, sin_y = jnp.zeros((8, PATCHES), jnp.float32), jnp.zeros((8, PATCHES), jnp.float32)
    for j, (c, s) in enumerate(
        [(1, 0), (root, root), (0, 1), (-root, root), (-1, 0), (-root, -root), (0, -1), (root, -root)]
    ):
        cos_y = jnp.where(angle == j, c, cos_y)
        sin_y = jnp.where(angle == j, s, sin_y)
    for plane in range(2):
        for k in range(5):
            source, first = (defl_ref, k * 32) if k < 2 else (shear_ref, (k - 2) * 32)
            cells = source[0, plane, first : first + 32, :].astype(jnp.float32) * (1.0 / 32.0)
            r0, r1, r2, r3 = [cells[i * 8 : i * 8 + 8] for i in range(4)]
            for a, part in enumerate((r0 + r1 + r2 + r3, r0 - r2, r1 - r3)):
                row = plane * ROWS + k * 9 + a * 3
                out_ref[row : row + 1, :] = jnp.sum(part, axis=0, keepdims=True)
                out_ref[row + 1 : row + 2, :] = jnp.sum(part * cos_y, axis=0, keepdims=True)
                out_ref[row + 2 : row + 3, :] = jnp.sum(part * sin_y, axis=0, keepdims=True)
        out_ref[plane * ROWS + 45 : plane * ROWS + 48, :] = jnp.zeros((3, PATCHES), jnp.float32)


def coefficients(deflection, shear):
    return pl.pallas_call(
        coefficients_kernel,
        out_shape=jax.ShapeDtypeStruct((2 * ROWS, PATCHES), jnp.float32),
        in_specs=[pl.BlockSpec(memory_space=pltpu.HBM)] * 2,
        out_specs=VMEM,
        scratch_shapes=[
            pltpu.VMEM(deflection.shape, deflection.dtype),
            pltpu.VMEM(shear.shape, shear.dtype),
            pltpu.SemaphoreType.DMA,
            pltpu.SemaphoreType.DMA,
        ],
        compiler_params=SMALL,
        name="coefficients",
    )(*[pltpu.with_memory_space_constraint(a, pltpu.HBM) for a in (deflection, shear)])


def join_kernel(count, *refs):
    out_ref, place = refs[-1], 0
    for ref in refs[:count]:
        out_ref[place : place + ref.shape[0]] = ref[...]
        place += ref.shape[0]


def join(blocks, after=()):
    shape = (sum(b.shape[0] for b in blocks), *blocks[0].shape[1:])
    return pl.pallas_call(
        functools.partial(join_kernel, len(blocks)),
        out_shape=jax.ShapeDtypeStruct(shape, blocks[0].dtype),
        in_specs=[VMEM] * (len(blocks) + len(after)),
        out_specs=VMEM,
        compiler_params=SMALL,
        name="join",
    )(*blocks, *after)


def fill_table(sources, table_ref, count):
    place = 0
    for ref in sources:
        for block in range(max(0, ref.shape[0] - count), ref.shape[0]):
            for plane in range(2):
                values = ref[block, plane * ROWS : (plane + 1) * ROWS, :]
                high = values.astype(jnp.bfloat16)
                low = (values - high.astype(jnp.float32)).astype(jnp.bfloat16)
                table_ref[plane, place * 2 * ROWS : place * 2 * ROWS + ROWS, :] = high
                table_ref[plane, place * 2 * ROWS + ROWS : (place + 1) * 2 * ROWS, :] = low
            place += 1


def find_rows(hop, tiles, table_ref, rel_ref, patch_ref, out_ref, before_ref=None):
    for plane in range(2):
        for chunk in range(RAYS // CHUNK):
            lanes = slice(chunk * CHUNK, (chunk + 1) * CHUNK)
            row = hop * 2 + plane
            patch = patch_ref[row : row + 1, lanes]
            rel = rel_ref[row : row + 1, lanes]
            onehot = lax.broadcasted_iota(jnp.int32, (PATCHES, CHUNK), 0) == patch
            onehot = jnp.where(onehot, 1.0, 0.0).astype(jnp.bfloat16)
            found = jnp.dot(table_ref[plane, : len(tiles) * 2 * ROWS], onehot, preferred_element_type=jnp.float32)
            total = [jnp.zeros((8, CHUNK), jnp.float32) for _ in range(ROWS // 8)]
            wide = jnp.broadcast_to(rel, (8, CHUNK))
            for place, tile in enumerate(tiles):
                here = wide == tile
                for part in range(ROWS // 8):
                    first = place * 2 * ROWS + part * 8
                    both = found[first : first + 8] + found[first + ROWS : first + ROWS + 8]
                    total[part] = total[part] + jnp.where(here, both, 0.0)
            for part in range(ROWS // 8):
                for half in range(CHUNK // 128):
                    group = chunk * (CHUNK // 128) + half
                    first = (plane * ROWS + part * 8) * GROUPS + group
                    place = pl.ds(first, 8, stride=GROUPS)
                    sums = total[part][:, half * 128 : half * 128 + 128]
                    out_ref[place, :] = sums if before_ref is None else sums + before_ref[place, :]


def table_kernel(*refs):
    fill_table(refs[:-1], refs[-1], TILES)


def table_of(sources):
    count = sum(source.shape[0] for source in sources)
    return pl.pallas_call(
        table_kernel,
        out_shape=jax.ShapeDtypeStruct((2, count * 2 * ROWS, PATCHES), jnp.bfloat16),
        in_specs=[VMEM] * len(sources),
        out_specs=VMEM,
        compiler_params=LARGE,
        name="table",
    )(*sources)


def lookup_kernel(hops, tiles, count, blocks, added, *refs):
    sources, (rel_ref, patch_ref), refs = refs[:count], refs[count : count + 2], refs[count + 2 :]
    before = refs[: len(hops)] if added else [None] * len(hops)
    outs = refs[-len(hops) :]
    if blocks:
        *outs, table_ref = refs[-1 - len(hops) :]
        fill_table(sources, table_ref, blocks)
    else:
        (table_ref,) = sources
    for hop, before_ref, out_ref in zip(hops, before, outs, strict=True):
        find_rows(hop, tiles, table_ref, rel_ref, patch_ref, out_ref, before_ref)


FOUND = jax.ShapeDtypeStruct((2 * ROWS * GROUPS, 128), jnp.float32)


COSTLY = pl.CostEstimate(flops=16000000000, bytes_accessed=100000, transcendentals=0)
COST = pl.CostEstimate(flops=100000, bytes_accessed=100000, transcendentals=0)


def scratch_table(tiles):
    return pltpu.VMEM((2, len(tiles) * 2 * ROWS, PATCHES), jnp.bfloat16)


def lookup(hops, tiles, sources, rel, patch, before=(), blocks=TILES):
    first = len(sources) + 2
    return pl.pallas_call(
        functools.partial(lookup_kernel, hops, tiles, len(sources), blocks, bool(before)),
        out_shape=[FOUND] * len(hops),
        in_specs=[VMEM] * (first + len(before)),
        out_specs=[VMEM] * len(hops),
        input_output_aliases={first + i: i for i in range(len(before))},
        scratch_shapes=[scratch_table(tiles)] if blocks else [],
        compiler_params=LARGE,
        cost_estimate=COSTLY if blocks else COST,
        name="lookup",
    )(*sources, rel, patch, *before)


def sine(turn):
    v = turn * (2.0 * math.pi)
    v2 = v * v
    poly = 1.0 / 6227020800.0
    for c in (-1.0 / 39916800.0, 1.0 / 362880.0, -1.0 / 5040.0, 1.0 / 120.0, -1.0 / 6.0):
        poly = poly * v2 + c
    return v + v * v2 * poly


def wave(turns):
    t = turns - jnp.floor(turns + 0.5)
    size = jnp.abs(t)
    fold = jnp.where(t >= 0, 0.5 - t, -0.5 - t)
    return sine(0.25 - size), sine(jnp.where(size > 0.25, fold, t))


def advance(state, read):
    pos_x, pos_y, ang_x, ang_y, a11, a12, a21, a22, b11, b12, b21, b22 = state
    cos_x, sin_x = wave(pos_x * 0.25)
    cos_y, sin_y = wave(pos_y * 0.125)
    values = []
    for k in range(5):
        parts = []
        for a in range(3):
            m = [read(k * 9 + a * 3 + b) for b in range(3)]
            parts.append(m[0] + m[1] * cos_y + m[2] * sin_y)
        values.append(parts[0] + parts[1] * cos_x + parts[2] * sin_x)
    alpha_x, alpha_y, psi11, psi12, psi22 = values
    ang_x = ang_x - alpha_x
    ang_y = ang_y - alpha_y
    b11 = b11 - (psi11 * a11 + psi12 * a21)
    b12 = b12 - (psi11 * a12 + psi12 * a22)
    b21 = b21 - (psi12 * a11 + psi22 * a21)
    b22 = b22 - (psi12 * a12 + psi22 * a22)
    pos_x = pos_x + 0.5 * ang_x
    pos_y = pos_y + 0.5 * ang_y
    a11 = a11 + 0.5 * b11
    a12 = a12 + 0.5 * b12
    a21 = a21 + 0.5 * b21
    a22 = a22 + 0.5 * b22
    return [pos_x, pos_y, ang_x, ang_y, a11, a12, a21, a22, b11, b12, b21, b22]


def rows(ref, k):
    return ref[k * GROUPS : (k + 1) * GROUPS, :]


def both_planes(state, read):
    for plane in range(2):
        state = advance(state, lambda k, plane=plane: read(plane * ROWS + k))
    return state


def summed(refs, k):
    return functools.reduce(jnp.add, [rows(ref, k) for ref in refs])


def first_step_kernel(tiles, parts, table_ref, rel_ref, patch_ref, state_ref, *refs):
    part_refs, (out_ref, leaving_ref, found_ref) = refs[:parts], refs[-3:]
    find_rows(0, tiles, table_ref, rel_ref, patch_ref, found_ref)
    found = (*part_refs, found_ref)
    state = both_planes([rows(state_ref, k) for k in range(12)], lambda k: summed(found, k))
    for k in range(12):
        out_ref[k * GROUPS : (k + 1) * GROUPS, :] = state[k]
        leaving_ref[k * GROUPS : (k + 1) * GROUPS, :] = state[k]


MOVED = jax.ShapeDtypeStruct((12 * GROUPS, 128), jnp.float32)
CROSSING = (100,108,108,204)


def moved_out(senders, step):
    return jax.ShapeDtypeStruct((CROSSING[step], 128), jnp.float32) if senders else MOVED


def first_step(tiles, table, rel, patch, state, parts):
    return pl.pallas_call(
        functools.partial(first_step_kernel, tiles, len(parts)),
        out_shape=[MOVED, moved_out(True, 0)],
        in_specs=[VMEM] * (4 + len(parts)),
        out_specs=[VMEM] * 2,
        scratch_shapes=[pltpu.VMEM(FOUND.shape, FOUND.dtype)],
        compiler_params=LARGE,
        cost_estimate=COST,
        name="first_step",
    )(table, rel, patch, state, *parts)


def step_kernel(senders, step, counts, q_ref, *refs):
    out_ref = refs[-1]
    main_ref, *refs = refs[: sum(counts)]
    wrap_ref = refs.pop(0) if counts[1] else None
    early, late = refs[: counts[2]], refs[counts[2] :]
    q = q_ref[0]
    shape = (GROUPS, 128)

    @pl.when((q == RUN - 1) == senders)
    def _():
        behind = jnp.full(shape, q, jnp.int32) < step
        crossed = jnp.full(shape, q, jnp.int32) == 0
        state = [rows(main_ref, k) for k in range(12)]
        if wrap_ref is not None and step > 1:
            state = [jnp.where(crossed, rows(wrap_ref, k), state[k]) for k in range(12)]

        def read(k):
            if not early:
                return summed(late, k)
            if not late:
                return summed(early, k)
            return jnp.where(behind, summed(late, k), summed(early, k))

        state = both_planes(state, read)
        if wrap_ref is not None and step == 1:
            state = [jnp.where(crossed, rows(wrap_ref, k), state[k]) for k in range(12)]
        for k in range(12):
            out_ref[k * GROUPS : (k + 1) * GROUPS, :] = state[k]


def run_step(senders, step, q, main, wrap, found, after=()):
    crossed = [] if senders else [wrap]
    early = found[step : step + 1]
    late = found[step - 1 : step] if step >= 2 and not senders else []
    args = [main, *crossed, *early, *late]
    return pl.pallas_call(
        functools.partial(step_kernel, senders, step, (1, len(crossed), len(early), len(late))),
        out_shape=moved_out(senders, step),
        in_specs=[SMEM] + [VMEM] * (len(args) + len(after)),
        out_specs=VMEM,
        compiler_params=SMALL,
        cost_estimate=COST,
        name="step",
    )(q, *args, *after)


RUN = 8


def tiles_of(masks, core):
    return tuple(m * 8 + j * 2 + core for m in masks for j in range(4))


def mixed(axis_first, axis_second):
    pairs = []
    for s in range(TILES):
        mask = axis_first if s % 2 == 0 else axis_second
        pairs.append((s, s ^ (mask << 3)))
    return pairs


def body(state, deflection, shear, routes, patches):
    slabs = lax.axis_size("los")
    slab = lax.axis_index("los")
    q = (slab % RUN).astype(jnp.int32).reshape(1)
    across = [(i, (i + 1) % slabs) for i in range(slabs) if i % RUN == RUN - 1]

    def onward(step):
        idle = {step} if step < HOPS else set(range(HOPS, RUN))
        return [(i, i + 1) for i in range(slabs) if i % RUN != RUN - 1 and i % RUN not in idle]

    route, patch = routes.reshape(2 * HOPS, RAYS), patches.reshape(2 * HOPS, RAYS)
    rel = jnp.bitwise_xor(route, lax.axis_index("sky").astype(jnp.int32))
    rel = jnp.bitwise_xor(rel, ((rel >> 3) & route & 1) << 4)
    rays = state.reshape(12 * GROUPS, 128)

    own = coefficients(deflection, shear)
    column = [own] + [lax.ppermute(own, "sky", partner("z", m)) for m in (1, 2, 3)]
    column = join([block[None] for block in column], [rel, patch, rays])
    near = [lax.ppermute(column, "sky", mixed(1, 3)), lax.ppermute(column, "sky", mixed(3, 1))]
    far = lax.ppermute(column, "sky", partner("x", 2))

    hops = range(HOPS)
    chip = partner("core", 1)
    mirror = lax.ppermute(join([column], near[:1]), "sky", chip)
    found = lookup(hops, tiles_of((0, 1), 0), [column, near[0]], rel, patch)
    found = lookup(hops, tiles_of((3,), 0) + tiles_of((0,), 1), [near[1], mirror], rel, patch, found)
    other = lax.ppermute(join([*near, far], found), "sky", chip)
    found = list(lookup(hops, tiles_of((2,), 0), [far], rel, patch, found))
    there = tiles_of((1, 3, 2), 1)
    other = table_of([other])
    moved, leaving = first_step(there, other, rel, patch, rays, found[:1])
    wraps, kept = [lax.ppermute(leaving, "los", across)], moved
    main, before = lax.ppermute(moved, "los", onward(0)), None
    for step in range(1, HOPS + 1):
        if step < HOPS:
            (found[step],) = lookup([step], there, [other], rel, patch, found[step : step + 1], 0)
        after = ()
        if step < HOPS:
            leaving = run_step(True, step, q, main, None, found)
            wraps.append(lax.ppermute(leaving, "los", across))
            after = (leaving,)
        moved = run_step(False, step, q, main, wraps[step - 2] if step >= 2 else kept, found, after)
        main, before = lax.ppermute(moved, "los", onward(step)), main
    out = jnp.where(q[0] == 0, wraps[HOPS - 1][:96], jnp.where(q[0] <= HOPS, main, before))
    return out.reshape(12, RAYS)


def solution(mesh):
    placed = (
        P(None, ("los", "sky")),
        P("los", None, None, "sky"),
        P("los", None, None, "sky"),
        P(None, None, ("los", "sky"), None),
        P(None, None, ("los", "sky")),
    )
    return jax.shard_map(
        body, mesh=mesh, in_specs=placed, out_specs=P(None, ("los", "sky")), check_vma=False
    )
```
